32 devices in a mesh: dp: 8 (over z, core), mp: 4 (over y, x).
Axes of the slice: x: 2, y: 2, z: 4, core: 2. Of those that a mesh axis runs over, the one named last changes fastest.
Arguments:
- inputs: bfloat16 [1024, 6144], P('dp', 'mp'), may hold values from -6 to 6
- up_weight: bfloat16 [4, 3, 24, 128, 128], P('mp'), may hold values from -0.3125 to 0.3125
- up_pick: int32 [4, 3, 24], P('mp'), may hold values from 0 to 11
- down_weight: bfloat16 [4, 3, 12, 2, 128, 128], P('mp'), may hold values from -0.21875 to 0.21875
- down_pick: int32 [4, 3, 12, 2], P('mp'), may hold values from 0 to 23
- cotangent: bfloat16 [1024, 6144], P('dp', 'mp'), may hold values from -6 to 6
Outputs:
- output: bfloat16 [1024, 6144], P('dp', 'mp')
- input_grad: bfloat16 [1024, 6144], P('dp', 'mp')
- up_grad: bfloat16 [4, 3, 24, 128, 128], P('mp')
- down_grad: bfloat16 [4, 3, 12, 2, 128, 128], P('mp')
The draws below stay inside these ranges and needn't reach their ends.
All inputs are finite; a program needn't handle non-finite values.
Results may differ from the reference program's by a relative error of at most 0.005.
Values may be sent and summed in bfloat16 or wider, within the bound.
A program may use at most 64 MiB of HBM per device.

```python
import math
import jax
import jax.numpy as jnp
import numpy as np
from jax import lax

D = 6144
BLOCK = 128
KD = 2
BITS = 2
LEVELS = 3
DB = 12
HB = 24
TOKENS = 1024
N_MP = 4


def set_ends(drawn, stream_key, smallest, high):
    spot = [jax.random.randint(jax.random.fold_in(stream_key, axis), (), 0, length) for axis, length in enumerate(drawn.shape)]
    main_axis = drawn.shape.index(max(drawn.shape))
    next_to = spot[:main_axis] + [(spot[main_axis] + 1) % drawn.shape[main_axis]] + spot[main_axis + 1:]
    return drawn.at[tuple(spot)].set(smallest).at[tuple(next_to)].set(high)


def level_of(rng, dims, pieces, low, largest):
    level = 1.0
    for axis_at, parts in pieces:
        steps = jax.random.uniform(jax.random.fold_in(jax.random.fold_in(rng, 6), axis_at), (parts,), jnp.float32, low / len(pieces), largest / len(pieces))
        level = level * jnp.repeat(jnp.exp(steps), dims[axis_at] // parts).reshape((-1,) + (1,) * (len(dims) - 1 - axis_at))
    return level


def normal_values(stream_key, extent, deviation, reach, cuts=(), kind=jnp.bfloat16):
    entries = deviation * jax.random.normal(stream_key, extent, jnp.float32)
    if cuts:
        entries = entries * level_of(stream_key, extent, cuts, -0.22, 0.18)
    return jnp.clip(entries, -reach, reach).astype(kind)


def setup_inputs(seed: int = 0) -> dict:
    key_list = jax.random.split(jax.random.key(seed), 7)
    return {
        "inputs": normal_values(key_list[0], (TOKENS, D), 1.0, 6.0, ((0, 8), (1, 4))),
        "up_weight": normal_values(key_list[1], (N_MP, LEVELS, HB, BLOCK, BLOCK), (LEVELS * BLOCK) ** -0.5, 0.3125, ((0, 4),)),
        "up_pick": set_ends(jax.random.randint(key_list[2], (N_MP, LEVELS, HB), 0, DB), jax.random.fold_in(key_list[2], 1), 0, DB - 1).astype(jnp.int32),
        "down_weight": normal_values(key_list[3], (N_MP, LEVELS, DB, KD, BLOCK, BLOCK), (LEVELS * KD * BLOCK) ** -0.5, 0.21875, ((0, 4),)),
        "down_pick": set_ends(jax.random.randint(key_list[4], (N_MP, LEVELS, DB, KD), 0, HB), jax.random.fold_in(key_list[4], 1), 0, HB - 1).astype(jnp.int32),
        "cotangent": normal_values(key_list[5], (TOKENS, D), 1.0, 6.0, ((0, 8), (1, 4))),
    }


def partner_ids():
    shard_ids = np.arange(N_MP, dtype=np.int32)[:, None]
    offsets = np.concatenate([np.zeros((1,), np.int32), (2 ** np.arange(BITS)).astype(np.int32)])
    return jnp.asarray((shard_ids ^ offsets[None, :]).astype(np.int32))

def up_map(inputs_f, weights_f, up_pick, partners):
    row_count = inputs_f.shape[0]
    blocks = inputs_f.reshape(row_count, N_MP, DB, BLOCK)
    hidden = jnp.zeros((row_count, N_MP, HB, BLOCK), jnp.float32)
    for level_num in range(LEVELS):
        chosen = blocks[:, partners[:, level_num][:, None], up_pick[:, level_num], :]
        hidden = hidden + jnp.einsum('tsob,sobc->tsoc', chosen, weights_f[:, level_num], precision=lax.Precision.HIGHEST)
    return hidden

def down_map(act_in, weights_f, down_pick, partners):
    row_count = act_in.shape[0]
    blocks = act_in.reshape(row_count, N_MP, HB, BLOCK)
    result = jnp.zeros((row_count, N_MP, DB, BLOCK), jnp.float32)
    for level_num in range(LEVELS):
        for slot_num in range(KD):
            chosen = blocks[:, partners[:, level_num][:, None], down_pick[:, level_num, :, slot_num], :]
            result = result + jnp.einsum('tsob,sobc->tsoc', chosen, weights_f[:, level_num, :, slot_num], precision=lax.Precision.HIGHEST)
    return result

def gelu_tanh(values_in):
    return jax.nn.gelu(values_in, approximate=True)

def reference(inputs, up_weight, up_pick, down_weight, down_pick, cotangent):
    partners = partner_ids()
    up_f = up_weight.astype(jnp.float32)
    down_f = down_weight.astype(jnp.float32)
    block_rows = math.gcd(TOKENS, 1024)
    steps_count = TOKENS // block_rows

    def one_block(running, block_pair):
        inputs_blk, cot_blk = block_pair
        hidden, up_back = jax.vjp(lambda inputs_f, weights_f: up_map(inputs_f, weights_f, up_pick, partners), inputs_blk.astype(jnp.float32), up_f)
        activation = gelu_tanh(hidden).astype(jnp.bfloat16)
        act_f = lax.optimization_barrier(activation).astype(jnp.float32)
        result, down_back = jax.vjp(lambda act_in, weights_f: down_map(act_in, weights_f, down_pick, partners), act_f, down_f)
        act_grad, grad_down = down_back(cot_blk.astype(jnp.float32).reshape(block_rows, N_MP, DB, BLOCK))
        _, gelu_back = jax.vjp(gelu_tanh, hidden)
        hidden_grad = gelu_back(act_grad)[0].astype(jnp.bfloat16)
        hidden_grad_f = lax.optimization_barrier(hidden_grad).astype(jnp.float32)
        grad_inputs, grad_up = up_back(hidden_grad_f)
        out_blk = result.reshape(block_rows, D).astype(jnp.bfloat16)
        return ((running[0] + grad_up, running[1] + grad_down), (out_blk, grad_inputs.astype(jnp.bfloat16)))
    start_sums = (jnp.zeros(up_weight.shape, jnp.float32), jnp.zeros(down_weight.shape, jnp.float32))
    (up_sum, down_sum), (out_all, dx_all) = lax.scan(one_block, start_sums, (inputs.reshape(steps_count, block_rows, D), cotangent.reshape(steps_count, block_rows, D)))
    grad_scale = 1.0 / math.sqrt(TOKENS)
    return (out_all.reshape(TOKENS, D), dx_all.reshape(TOKENS, D), (up_sum * grad_scale).astype(jnp.bfloat16), (down_sum * grad_scale).astype(jnp.bfloat16))
```

```python
import functools
import math

import jax
import jax.numpy as jnp
from jax import lax
from jax.experimental import pallas as pl
from jax.experimental.pallas import tpu as pltpu
from jax.sharding import PartitionSpec as P

F32 = jnp.float32
BF16 = jnp.bfloat16
VM = pl.BlockSpec(memory_space=pltpu.VMEM)
SM = pl.BlockSpec(memory_space=pltpu.SMEM)


def dot(a, b, dims):
    return lax.dot_general(a, b, (dims, ((), ())), preferred_element_type=F32)


def call(body, outs, flops, moved, in_specs, scratch=()):
    return pl.pallas_call(
        body,
        out_shape=[jax.ShapeDtypeStruct(s, d) for s, d in outs],
        in_specs=in_specs,
        out_specs=[VM] * len(outs),
        scratch_shapes=list(scratch),
        compiler_params=pltpu.CompilerParams(vmem_limit_bytes=48 * 2**20),
        cost_estimate=pl.CostEstimate(flops=flops, bytes_accessed=moved, transcendentals=0),
    )


def columns(block, size):
    return pl.ds(pl.multiple_of(block * size, size), size)


def back_body(levels, pick, dy, weight, *rest):
    outs, total = rest[:levels], rest[levels]
    _, _, out_blocks, slots, size, _ = weight.shape
    total[...] = jnp.zeros_like(total)

    @pl.loop(0, out_blocks)
    def _(o):
        grad = dy[:, columns(o, size)]
        terms = [
            (l, k, dot(grad, weight[0, l, o, k], ((1,), (1,))))
            for l in range(levels)
            for k in range(slots)
        ]
        for l, k, term in terms:
            spot = pick[0, l, o, k]
            total[l, spot] += term

    for l in range(levels):
        outs[l][...] = total[l].astype(outs[l].dtype)


def gelu_parts(v):
    c = 0.7978845608028654
    t = jnp.tanh(c * (v + 0.044715 * (v * v * v)))
    return t, c


def up_body(levels, pick, *rest):
    sources, weight, hidden, act = rest[:levels], rest[levels], rest[levels + 1], rest[levels + 2]
    hid_blocks, size = weight.shape[2], weight.shape[3]

    def one(o):
        acc = None
        for l in range(levels):
            block = sources[l][:, columns(pick[0, l, o], size)]
            term = dot(block, weight[0, l, o], ((1,), (0,)))
            acc = term if acc is None else acc + term
        t, _ = gelu_parts(acc)
        hidden[o] = acc
        act[o] = (0.5 * acc * (1.0 + t)).astype(BF16)

    @pl.loop(0, hid_blocks // 3)
    def _(step):
        for i in range(3):
            one(step * 3 + i)


def mid_body(levels, pick, *rest):
    sources = rest[:levels]
    weight, hidden = rest[levels], rest[levels + 1]
    grads = rest[levels + 2 : 2 * levels + 2]
    up_part = rest[2 * levels + 2]
    outs = rest[2 * levels + 3 : 3 * levels + 3]
    total, flipped = rest[3 * levels + 3 :]
    hid_blocks, size = weight.shape[2], weight.shape[3]
    in_blocks = sources[0].shape[1] // size
    total[...] = jnp.zeros_like(total)

    @pl.loop(0, in_blocks)
    def _(b):
        for l in range(levels):
            flipped[l, b] = sources[l][:, columns(b, size)].T

    def one(o):
        v = hidden[o]
        grad = grads[0][o]
        for l in range(1, levels):
            grad = grad + grads[l][o].astype(F32)
        t, c = gelu_parts(v)
        slope = 0.5 * (1.0 + t) + 0.5 * v * (1.0 - t * t) * (c * (1.0 + 3 * 0.044715 * (v * v)))
        hg = (grad * slope).astype(BF16)
        terms = []
        for l in range(levels):
            up_part[l, o] = dot(flipped[l, pick[0, l, o]], hg, ((1,), (0,))).astype(BF16)
            terms.append(dot(hg, weight[0, l, o], ((1,), (1,))))
        return terms

    @pl.loop(0, hid_blocks // 2)
    def _(step):
        both = [one(step * 2 + i) for i in range(2)]
        for i in range(2):
            for l in range(levels):
                spot = pick[0, l, step * 2 + i]
                total[l, spot] += both[i][l]

    for l in range(levels):
        outs[l][...] = total[l].astype(outs[l].dtype)


def down_body(levels, pick, *rest):
    acts, weight, dy, result, down_part = rest[:levels], *rest[levels:]
    _, _, out_blocks, slots, size, _ = weight.shape

    @pl.loop(0, out_blocks)
    def _(o):
        grad = dy[:, columns(o, size)]
        acc = None
        for l in range(levels):
            for k in range(slots):
                act = acts[l][pick[0, l, o, k]]
                term = dot(act, weight[0, l, o, k], ((1,), (0,)))
                acc = term if acc is None else acc + term
                down_part[l, o, k] = dot(act, grad, ((0,), (0,))).astype(BF16)
        result[:, columns(o, size)] = acc.astype(BF16)


def sum_body(levels, *rest):
    terms, out = rest[:levels], rest[levels]
    blocks, _, size = terms[0].shape

    for b in range(blocks):
        acc = terms[0][b]
        for l in range(1, levels):
            acc = acc + terms[l][b].astype(F32)
        out[:, b * size : (b + 1) * size] = acc.astype(BF16)


def swap(block, axis, bit):
    count = lax.axis_size(axis)
    return lax.ppermute(block, axis, [(i, i ^ (1 << bit)) for i in range(count)])


def token_sum(part, scale):
    me = lax.axis_index("dp")
    bits = lax.axis_size("dp").bit_length() - 1
    value = part.reshape(-1, part.shape[-1])
    for bit in range(bits):
        mine = (me >> bit) & 1
        rows = value.shape[0] // 2
        sent = lax.dynamic_slice_in_dim(value, (1 - mine) * rows, rows).astype(BF16)
        kept = lax.dynamic_slice_in_dim(value, mine * rows, rows).astype(F32)
        value = kept + swap(sent, "dp", bit).astype(F32)
    value = (value * scale).astype(BF16)
    for bit in reversed(range(bits)):
        mine = (me >> bit) & 1
        other = swap(value, "dp", bit)
        first = jnp.where(mine == 0, value, other)
        last = jnp.where(mine == 0, other, value)
        value = jnp.concatenate([first, last], axis=0)
    return value.reshape((1,) + part.shape)


def local(inputs, up_weight, up_pick, down_weight, down_pick, cotangent):
    bit_count = lax.axis_size("mp").bit_length() - 1
    levels = bit_count + 1
    tokens, width = inputs.shape
    in_blocks, slots = down_weight.shape[2:4]
    hid_blocks, size = up_weight.shape[2:4]
    scale = 1.0 / math.sqrt(tokens * lax.axis_size("dp"))
    macs = 2 * levels * hid_blocks * tokens * size * size
    hid = (hid_blocks, tokens, size)
    feat = (in_blocks, tokens, size)

    sources = [inputs] + [swap(inputs, "mp", b) for b in range(bit_count)]
    placed = call(
        functools.partial(back_body, levels),
        [(hid, F32)] + [(hid, BF16)] * bit_count,
        macs, 8 * 2**20, [SM, VM, VM],
        [pltpu.VMEM((levels,) + hid, F32)],
    )(down_pick, cotangent, down_weight)
    grads = [placed[0]] + [swap(placed[b + 1], "mp", b) for b in range(bit_count)]
    hidden, act = call(
        functools.partial(up_body, levels),
        [(hid, F32), (hid, BF16)],
        macs, 8 * 2**20, [SM] + [VM] * (levels + 1),
    )(up_pick, *sources, up_weight)
    acts = [act] + [swap(act, "mp", b) for b in range(bit_count)]
    mid = call(
        functools.partial(mid_body, levels),
        [((levels, hid_blocks, size, size), BF16), (feat, F32)] + [(feat, BF16)] * bit_count,
        2 * macs, 16 * 2**20, [SM] + [VM] * (2 * levels + 2),
        [
            pltpu.VMEM((levels,) + feat, F32),
            pltpu.VMEM((levels, in_blocks, size, tokens), BF16),
        ],
    )(up_pick, *sources, up_weight, hidden, *grads)
    up_part, back = mid[0], mid[1:]
    result, down_part = call(
        functools.partial(down_body, levels),
        [((tokens, width), BF16), ((levels, in_blocks, slots, size, size), BF16)],
        2 * macs, 12 * 2**20, [SM] + [VM] * (levels + 2),
    )(down_pick, *acts, down_weight, cotangent)
    backs = [back[0]] + [swap(back[b + 1], "mp", b) for b in range(bit_count)]
    up_out = token_sum(up_part, scale)
    down_out = token_sum(down_part, scale)
    [grad_inputs] = call(
        functools.partial(sum_body, levels),
        [((tokens, width), BF16)], 2**20, 2 * 2**20, [VM] * levels,
    )(*backs)
    return result, grad_inputs, up_out, down_out


def solution(mesh):
    placed = (
        P("dp", "mp"),
        P("mp", None, None, None, None),
        P("mp", None, None),
        P("mp", None, None, None, None, None),
        P("mp", None, None, None),
        P("dp", "mp"),
    )
    return jax.shard_map(
        local,
        mesh=mesh,
        in_specs=placed,
        out_specs=(
            P("dp", "mp"),
            P("dp", "mp"),
            P("mp", None, None, None, None),
            P("mp", None, None, None, None, None),
        ),
        check_vma=False,
    )
```

```python
import functools
import math

import jax
import jax.numpy as jnp
from jax import lax
from jax.experimental import pallas as pl
from jax.experimental.pallas import tpu as pltpu
from jax.sharding import PartitionSpec as P

F32 = jnp.float32
BF16 = jnp.bfloat16
VM = pl.BlockSpec(memory_space=pltpu.VMEM)
SM = pl.BlockSpec(memory_space=pltpu.SMEM)


def dot(a, b, dims):
    return lax.dot_general(a, b, (dims, ((), ())), preferred_element_type=F32)


def call(body, outs, flops, moved, in_specs, scratch=()):
    return pl.pallas_call(
        body,
        out_shape=[jax.ShapeDtypeStruct(s, d) for s, d in outs],
        in_specs=in_specs,
        out_specs=[VM] * len(outs),
        scratch_shapes=list(scratch),
        compiler_params=pltpu.CompilerParams(vmem_limit_bytes=48 * 2**20),
        cost_estimate=pl.CostEstimate(flops=flops, bytes_accessed=moved, transcendentals=0),
    )


def columns(block, size):
    return pl.ds(pl.multiple_of(block * size, size), size)


def back_body(levels, pick, dy, weight, *rest):
    outs, total = rest[:levels], rest[levels]
    _, _, out_blocks, slots, size, _ = weight.shape
    total[...] = jnp.zeros_like(total)

    @pl.loop(0, out_blocks)
    def _(o):
        grad = dy[:, columns(o, size)]
        terms = [
            (l, k, dot(grad, weight[0, l, o, k], ((1,), (1,))))
            for l in range(levels)
            for k in range(slots)
        ]
        for l, k, term in terms:
            spot = pick[0, l, o, k]
            total[l, spot] += term

    for l in range(levels):
        outs[l][...] = total[l].astype(outs[l].dtype)


def gelu_parts(v):
    c = 0.7978845608028654
    t = jnp.tanh(c * (v + 0.044715 * (v * v * v)))
    return t, c


def up_body(levels, pick, *rest):
    sources, weight, hidden, act = rest[:levels], rest[levels], rest[levels + 1], rest[levels + 2]
    hid_blocks, size = weight.shape[2], weight.shape[3]

    def one(o):
        acc = None
        for l in range(levels):
            block = sources[l][:, columns(pick[0, l, o], size)]
            term = dot(block, weight[0, l, o], ((1,), (0,)))
            acc = term if acc is None else acc + term
        t, _ = gelu_parts(acc)
        hidden[o] = acc
        act[o] = (0.5 * acc * (1.0 + t)).astype(BF16)

    @pl.loop(0, hid_blocks // 3)
    def _(step):
        for i in range(3):
            one(step * 3 + i)


def mid_body(levels, pick, *rest):
    sources = rest[:levels]
    weight, hidden = rest[levels], rest[levels + 1]
    grads = rest[levels + 2 : 2 * levels + 2]
    up_part = rest[2 * levels + 2]
    outs = rest[2 * levels + 3 : 3 * levels + 3]
    total, flipped = rest[3 * levels + 3 :]
    hid_blocks, size = weight.shape[2], weight.shape[3]
    in_blocks = sources[0].shape[1] // size
    total[...] = jnp.zeros_like(total)

    @pl.loop(0, in_blocks)
    def _(b):
        for l in range(levels):
            flipped[l, b] = sources[l][:, columns(b, size)].T

    def one(o):
        v = hidden[o]
        grad = grads[0][o]
        for l in range(1, levels):
            grad = grad + grads[l][o].astype(F32)
        t, c = gelu_parts(v)
        slope = 0.5 * (1.0 + t) + 0.5 * v * (1.0 - t * t) * (c * (1.0 + 3 * 0.044715 * (v * v)))
        hg = (grad * slope).astype(BF16)
        terms = []
        for l in range(levels):
            up_part[l, o] = dot(flipped[l, pick[0, l, o]], hg, ((1,), (0,))).astype(BF16)
            terms.append(dot(hg, weight[0, l, o], ((1,), (1,))))
        return terms

    @pl.loop(0, hid_blocks // 2)
    def _(step):
        both = [one(step * 2 + i) for i in range(2)]
        for i in range(2):
            for l in range(levels):
                spot = pick[0, l, step * 2 + i]
                total[l, spot] += both[i][l]

    for l in range(levels):
        outs[l][...] = total[l].astype(outs[l].dtype)


def down_body(levels, pick, *rest):
    acts, weight, dy, result, down_part = rest[:levels], *rest[levels:]
    _, _, out_blocks, slots, size, _ = weight.shape

    @pl.loop(0, out_blocks)
    def _(o):
        grad = dy[:, columns(o, size)]
        acc = None
        for l in range(levels):
            for k in range(slots):
                act = acts[l][pick[0, l, o, k]]
                term = dot(act, weight[0, l, o, k], ((1,), (0,)))
                acc = term if acc is None else acc + term
                down_part[l, o, k] = dot(act, grad, ((0,), (0,))).astype(BF16)
        result[:, columns(o, size)] = acc.astype(BF16)


def sum_body(levels, *rest):
    terms, out = rest[:levels], rest[levels]
    blocks, _, size = terms[0].shape

    for b in range(blocks):
        acc = terms[0][b]
        for l in range(1, levels):
            acc = acc + terms[l][b].astype(F32)
        out[:, b * size : (b + 1) * size] = acc.astype(BF16)


def swap(block, axis, bit):
    count = lax.axis_size(axis)
    return lax.ppermute(block, axis, [(i, i ^ (1 << bit)) for i in range(count)])


def token_sum(part, scale):
    me = lax.axis_index("dp")
    bits = lax.axis_size("dp").bit_length() - 1
    value = part.reshape(-1, part.shape[-1])
    for bit in range(bits):
        mine = (me >> bit) & 1
        rows = value.shape[0] // 2
        sent = lax.dynamic_slice_in_dim(value, (1 - mine) * rows, rows).astype(BF16)
        kept = lax.dynamic_slice_in_dim(value, mine * rows, rows).astype(F32)
        value = kept + swap(sent, "dp", bit).astype(F32)
    value = (value * scale).astype(BF16)
    for bit in reversed(range(bits)):
        mine = (me >> bit) & 1
        other = swap(value, "dp", bit)
        first = jnp.where(mine == 0, value, other)
        last = jnp.where(mine == 0, other, value)
        value = jnp.concatenate([first, last], axis=0)
    return value.reshape((1,) + part.shape)


def stream_count(rows, devices):
    return next((n for n in (4, 2, 1) if rows % (16 * devices * n) == 0), 0)


def sum_streams_body(count, streams, bits, scale, *refs):
    parts, outs = refs[:count], refs[count : 2 * count]
    acc, stage, land, send_sem, recv_sem = refs[2 * count :]
    me = lax.axis_index("dp")
    mine = [lax.rem(lax.div(me, 1 << b), 2) for b in range(bits)]
    peer = [me + (1 - 2 * mine[b]) * (1 << b) for b in range(bits)]
    rows = parts[0].shape[0] // streams
    size = [rows >> (b + 1) for b in range(bits)]
    total = count * streams

    barrier = pltpu.get_barrier_semaphore()
    for b in range(bits):
        pl.semaphore_signal(
            barrier, inc=1, device_id={"dp": peer[b]}, device_id_type=pl.DeviceIdType.MESH
        )
    pl.semaphore_wait(barrier, bits)

    start = [0] * (bits + 1)
    for b in range(bits):
        start[b + 1] = start[b] + mine[b] * size[b]
    place = [0]
    for b in range(bits):
        place.append(place[b] + size[b])

    def span(at, length):
        return pl.ds(pl.multiple_of(at, 16), length)

    def copy(j, step):
        which, base = j // streams, (j % streams) * rows
        if step < bits:
            b = step
            there = start[b] + (1 - mine[b]) * size[b]
            source = (
                parts[which].at[span(base + there, size[0])]
                if b == 0
                else stage.at[j, pl.ds(place[b] - size[0], size[b])]
            )
            target = land.at[j, pl.ds(place[b], size[b])]
        else:
            b = 2 * bits - 1 - step
            source = target = outs[which].at[span(base + start[b + 1], size[b])]
        return pltpu.make_async_remote_copy(
            src_ref=source,
            dst_ref=target,
            send_sem=send_sem.at[j, step],
            recv_sem=recv_sem.at[j, step],
            device_id={"dp": peer[b]},
            device_id_type=pl.DeviceIdType.MESH,
        )

    def advance(j, step):
        which, base = j // streams, (j % streams) * rows
        if step > 0:
            copy(j, step - 1).wait_recv()
        if 0 < step <= bits:
            b = step - 1
            arrived = land[j, pl.ds(place[b], size[b])].astype(jnp.float32)
            if b == 0:
                held = parts[which][span(base + mine[0] * size[0], size[0])].astype(jnp.float32)
            else:
                held = acc[j, span(start[b + 1] - start[1], size[b])]
            value = held + arrived
            if step == bits:
                outs[which][span(base + start[bits], size[b])] = (value * scale).astype(jnp.bfloat16)
            else:
                acc[j, span(start[b + 1] - start[1], size[b])] = value
                away = start[step] - start[1] + (1 - mine[step]) * size[step]
                stage[j, pl.ds(place[step] - size[0], size[step])] = acc[
                    j, span(away, size[step])
                ].astype(jnp.bfloat16)
        if step < 2 * bits:
            copy(j, step).start()

    for tick in range(2 * bits + total):
        for j in range(total):
            if 0 <= tick - j <= 2 * bits:
                advance(j, tick - j)
    for j in range(total):
        for step in range(2 * bits):
            copy(j, step).wait_send()


def token_sums(parts, scale):
    devices = lax.axis_size("dp")
    bits = devices.bit_length() - 1
    flat = [p.reshape(-1, p.shape[-1]) for p in parts]
    height, width = flat[0].shape
    streams = stream_count(height, devices)
    if not streams or bits < 2 or any(f.shape != flat[0].shape for f in flat):
        return [token_sum(p, scale) for p in parts]
    count, rows = len(parts), height // streams
    total = count * streams
    moved = [rows >> (b + 1) for b in range(bits)]
    sums = pl.pallas_call(
        functools.partial(sum_streams_body, count, streams, bits, scale),
        out_shape=[jax.ShapeDtypeStruct(f.shape, BF16) for f in flat],
        in_specs=[VM] * count,
        out_specs=[VM] * count,
        scratch_shapes=[
            pltpu.VMEM((total, moved[0], width), F32),
            pltpu.VMEM((total, sum(moved[1:]), width), BF16),
            pltpu.VMEM((total, sum(moved), width), BF16),
            pltpu.SemaphoreType.DMA((total, 2 * bits)),
            pltpu.SemaphoreType.DMA((total, 2 * bits)),
        ],
        compiler_params=pltpu.CompilerParams(
            collective_id=0, has_side_effects=True, vmem_limit_bytes=48 * 2**20
        ),
        cost_estimate=pl.CostEstimate(flops=2**20, bytes_accessed=200 * 2**20, transcendentals=0),
    )(*flat)
    return [s.reshape((1,) + p.shape) for s, p in zip(sums, parts)]


def local(inputs, up_weight, up_pick, down_weight, down_pick, cotangent):
    bit_count = lax.axis_size("mp").bit_length() - 1
    levels = bit_count + 1
    tokens, width = inputs.shape
    in_blocks, slots = down_weight.shape[2:4]
    hid_blocks, size = up_weight.shape[2:4]
    scale = 1.0 / math.sqrt(tokens * lax.axis_size("dp"))
    macs = 2 * levels * hid_blocks * tokens * size * size
    hid = (hid_blocks, tokens, size)
    feat = (in_blocks, tokens, size)

    sources = [inputs] + [swap(inputs, "mp", b) for b in range(bit_count)]
    placed = call(
        functools.partial(back_body, levels),
        [(hid, F32)] + [(hid, BF16)] * bit_count,
        macs, 8 * 2**20, [SM, VM, VM],
        [pltpu.VMEM((levels,) + hid, F32)],
    )(down_pick, cotangent, down_weight)
    grads = [placed[0]] + [swap(placed[b + 1], "mp", b) for b in range(bit_count)]
    hidden, act = call(
        functools.partial(up_body, levels),
        [(hid, F32), (hid, BF16)],
        macs, 8 * 2**20, [SM] + [VM] * (levels + 1),
    )(up_pick, *sources, up_weight)
    acts = [act] + [swap(act, "mp", b) for b in range(bit_count)]
    mid = call(
        functools.partial(mid_body, levels),
        [((levels, hid_blocks, size, size), BF16), (feat, F32)] + [(feat, BF16)] * bit_count,
        2 * macs, 16 * 2**20, [SM] + [VM] * (2 * levels + 2),
        [
            pltpu.VMEM((levels,) + feat, F32),
            pltpu.VMEM((levels, in_blocks, size, tokens), BF16),
        ],
    )(up_pick, *sources, up_weight, hidden, *grads)
    up_part, back = mid[0], mid[1:]
    result, down_part = call(
        functools.partial(down_body, levels),
        [((tokens, width), BF16), ((levels, in_blocks, slots, size, size), BF16)],
        2 * macs, 12 * 2**20, [SM] + [VM] * (levels + 2),
    )(down_pick, *acts, down_weight, cotangent)
    backs = [back[0]] + [swap(back[b + 1], "mp", b) for b in range(bit_count)]
    up_out, down_out = token_sums([up_part, down_part], scale)
    [grad_inputs] = call(
        functools.partial(sum_body, levels),
        [((tokens, width), BF16)], 2**20, 2 * 2**20, [VM] * levels,
    )(*backs)
    return result, grad_inputs, up_out, down_out


def solution(mesh):
    placed = (
        P("dp", "mp"),
        P("mp", None, None, None, None),
        P("mp", None, None),
        P("mp", None, None, None, None, None),
        P("mp", None, None, None),
        P("dp", "mp"),
    )
    return jax.shard_map(
        local,
        mesh=mesh,
        in_specs=placed,
        out_specs=(
            P("dp", "mp"),
            P("dp", "mp"),
            P("mp", None, None, None, None),
            P("mp", None, None, None, None, None),
        ),
        check_vma=False,
    )
```

```python
import functools
import math

import jax
import jax.numpy as jnp
from jax import lax
from jax.experimental import pallas as pl
from jax.experimental.pallas import tpu as pltpu
from jax.sharding import PartitionSpec as P

F32 = jnp.float32
BF16 = jnp.bfloat16
VM = pl.BlockSpec(memory_space=pltpu.VMEM)
SM = pl.BlockSpec(memory_space=pltpu.SMEM)


def dot(a, b, dims):
    return lax.dot_general(a, b, (dims, ((), ())), preferred_element_type=F32)


def call(body, outs, flops, moved, in_specs, scratch=()):
    return pl.pallas_call(
        body,
        out_shape=[jax.ShapeDtypeStruct(s, d) for s, d in outs],
        in_specs=in_specs,
        out_specs=[VM] * len(outs),
        scratch_shapes=list(scratch),
        compiler_params=pltpu.CompilerParams(vmem_limit_bytes=48 * 2**20),
        cost_estimate=pl.CostEstimate(flops=flops, bytes_accessed=moved, transcendentals=0),
    )


def columns(block, size):
    return pl.ds(pl.multiple_of(block * size, size), size)


def back_body(levels, pick, dy, weight, *rest):
    outs, total = rest[:levels], rest[levels]
    _, _, out_blocks, slots, size, _ = weight.shape
    total[...] = jnp.zeros_like(total)

    @pl.loop(0, out_blocks)
    def _(o):
        grad = dy[:, columns(o, size)]
        terms = [
            (l, k, dot(grad, weight[0, l, o, k], ((1,), (1,))))
            for l in range(levels)
            for k in range(slots)
        ]
        for l, k, term in terms:
            spot = pick[0, l, o, k]
            total[l, spot] += term

    for l in range(levels):
        outs[l][...] = total[l].astype(outs[l].dtype)


def gelu_parts(v):
    c = 0.7978845608028654
    t = jnp.tanh(c * (v + 0.044715 * (v * v * v)))
    return t, c


def up_body(levels, pick, *rest):
    sources, weight, hidden, act = rest[:levels], rest[levels], rest[levels + 1], rest[levels + 2]
    hid_blocks, size = weight.shape[2], weight.shape[3]

    def one(o):
        acc = None
        for l in range(levels):
            block = sources[l][:, columns(pick[0, l, o], size)]
            term = dot(block, weight[0, l, o], ((1,), (0,)))
            acc = term if acc is None else acc + term
        t, _ = gelu_parts(acc)
        hidden[o] = acc
        act[o] = (0.5 * acc * (1.0 + t)).astype(BF16)

    @pl.loop(0, hid_blocks // 3)
    def _(step):
        for i in range(3):
            one(step * 3 + i)


def mid_body(levels, pick, *rest):
    sources = rest[:levels]
    weight, hidden = rest[levels], rest[levels + 1]
    grads = rest[levels + 2 : 2 * levels + 2]
    up_part = rest[2 * levels + 2]
    outs = rest[2 * levels + 3 : 3 * levels + 3]
    total, flipped = rest[3 * levels + 3 :]
    hid_blocks, size = weight.shape[2], weight.shape[3]
    in_blocks = sources[0].shape[1] // size
    total[...] = jnp.zeros_like(total)

    @pl.loop(0, in_blocks)
    def _(b):
        for l in range(levels):
            flipped[l, b] = sources[l][:, columns(b, size)].T

    def one(o):
        v = hidden[o]
        grad = grads[0][o]
        for l in range(1, levels):
            grad = grad + grads[l][o].astype(F32)
        t, c = gelu_parts(v)
        slope = 0.5 * (1.0 + t) + 0.5 * v * (1.0 - t * t) * (c * (1.0 + 3 * 0.044715 * (v * v)))
        hg = (grad * slope).astype(BF16)
        terms = []
        for l in range(levels):
            up_part[l, o] = dot(flipped[l, pick[0, l, o]], hg, ((1,), (0,))).astype(BF16)
            terms.append(dot(hg, weight[0, l, o], ((1,), (1,))))
        return terms

    @pl.loop(0, hid_blocks // 2)
    def _(step):
        both = [one(step * 2 + i) for i in range(2)]
        for i in range(2):
            for l in range(levels):
                spot = pick[0, l, step * 2 + i]
                total[l, spot] += both[i][l]

    for l in range(levels):
        outs[l][...] = total[l].astype(outs[l].dtype)


def down_body(levels, pick, *rest):
    acts, weight, dy, result, down_part = rest[:levels], *rest[levels:]
    _, _, out_blocks, slots, size, _ = weight.shape

    @pl.loop(0, out_blocks)
    def _(o):
        grad = dy[:, columns(o, size)]
        acc = None
        for l in range(levels):
            for k in range(slots):
                act = acts[l][pick[0, l, o, k]]
                term = dot(act, weight[0, l, o, k], ((1,), (0,)))
                acc = term if acc is None else acc + term
                down_part[l, o, k] = dot(act, grad, ((0,), (0,))).astype(BF16)
        result[:, columns(o, size)] = acc.astype(BF16)


def sum_body(levels, *rest):
    terms, out = rest[:levels], rest[levels]
    blocks, _, size = terms[0].shape

    for b in range(blocks):
        acc = terms[0][b]
        for l in range(1, levels):
            acc = acc + terms[l][b].astype(F32)
        out[:, b * size : (b + 1) * size] = acc.astype(BF16)


def swap(block, axis, bit):
    count = lax.axis_size(axis)
    return lax.ppermute(block, axis, [(i, i ^ (1 << bit)) for i in range(count)])


def token_sum(part, scale):
    me = lax.axis_index("dp")
    bits = lax.axis_size("dp").bit_length() - 1
    value = part.reshape(-1, part.shape[-1])
    for bit in range(bits):
        mine = (me >> bit) & 1
        rows = value.shape[0] // 2
        sent = lax.dynamic_slice_in_dim(value, (1 - mine) * rows, rows).astype(BF16)
        kept = lax.dynamic_slice_in_dim(value, mine * rows, rows).astype(F32)
        value = kept + swap(sent, "dp", bit).astype(F32)
    value = (value * scale).astype(BF16)
    for bit in reversed(range(bits)):
        mine = (me >> bit) & 1
        other = swap(value, "dp", bit)
        first = jnp.where(mine == 0, value, other)
        last = jnp.where(mine == 0, other, value)
        value = jnp.concatenate([first, last], axis=0)
    return value.reshape((1,) + part.shape)


LAGS = (0, 2, 4, 5, 7, 9, 11)


def stream_count(rows):
    return next((n for n in (8, 6, 4, 3, 2, 1) if rows % (64 * n) == 0), 0)


def sum_streams_body(count, streams, scale, *refs):
    parts, outs = refs[:count], refs[count : 2 * count]
    acc, stage, land_core, land_end, land_mid, send_sem, recv_sem = refs[2 * count :]
    me = lax.axis_index("dp")
    core = lax.rem(me, 2)
    z = lax.div(me, 2)
    inner = jnp.logical_or(z == 1, z == 2)
    end = jnp.logical_or(z == 0, z == 3)
    core_peer = me + 1 - 2 * core
    edge_peer = me + 2 - 4 * lax.rem(z, 2)
    mid_peer = me + 6 - 4 * z
    part_mid = lax.div(z, 2)
    half = parts[0].shape[0] // streams // 2
    quarter = half // 2
    total = count * streams
    mesh_id = pl.DeviceIdType.MESH

    barrier = pltpu.get_barrier_semaphore()
    for peer in (core_peer, edge_peer):
        pl.semaphore_signal(barrier, inc=1, device_id={"dp": peer}, device_id_type=mesh_id)

    @pl.when(inner)
    def _():
        pl.semaphore_signal(barrier, inc=1, device_id={"dp": mid_peer}, device_id_type=mesh_id)
        pl.semaphore_wait(barrier, 3)

    @pl.when(end)
    def _():
        pl.semaphore_wait(barrier, 2)

    def span(at, length):
        return pl.ds(pl.multiple_of(at, 16), length)

    def copy(j, kind):
        which, base = j // streams, (j % streams) * 2 * half
        own = span(base + core * half, half)
        if kind == 0:
            source = parts[which].at[span(base + (1 - core) * half, half)]
            target, peer = land_core.at[j], core_peer
        elif kind == 1:
            source, target, peer = stage.at[j], land_end.at[j], edge_peer
        elif kind == 2:
            source = stage.at[j, span((1 - part_mid) * quarter, quarter)]
            target, peer = land_mid.at[j], mid_peer
        elif kind == 3:
            source = outs[which].at[span(base + core * half + part_mid * quarter, quarter)]
            target, peer = source, mid_peer
        else:
            source = target = outs[which].at[own]
            peer = edge_peer if kind == 4 else core_peer
        return pltpu.make_async_remote_copy(
            src_ref=source,
            dst_ref=target,
            send_sem=send_sem.at[j, kind],
            recv_sem=recv_sem.at[j, kind],
            device_id={"dp": peer},
            device_id_type=mesh_id,
        )

    def advance(j, step):
        which, base = j // streams, (j % streams) * 2 * half
        if step == 0:
            copy(j, 0).start()
        elif step == 1:
            copy(j, 0).wait_recv()
            own = parts[which][span(base + core * half, half)].astype(F32)
            value = own + land_core[j].astype(F32)

            @pl.when(end)
            def _():
                stage[j] = value.astype(BF16)
                copy(j, 1).start()

            @pl.when(inner)
            def _():
                acc[j] = value

        elif step == 2:

            @pl.when(inner)
            def _():
                copy(j, 1).wait_recv()
                value = acc[j] + land_end[j].astype(F32)
                acc[j] = value
                stage[j] = value.astype(BF16)
                copy(j, 2).start()

        elif step == 3:

            @pl.when(inner)
            def _():
                copy(j, 2).wait_recv()
                held = acc[j, span(part_mid * quarter, quarter)]
                value = held + land_mid[j].astype(F32)
                place = span(base + core * half + part_mid * quarter, quarter)
                outs[which][place] = (value * scale).astype(BF16)
                copy(j, 3).start()

        elif step == 4:

            @pl.when(inner)
            def _():
                copy(j, 3).wait_recv()
                copy(j, 4).start()
                copy(j, 5).start()

        elif step == 5:

            @pl.when(end)
            def _():
                copy(j, 4).wait_recv()
                copy(j, 5).start()

        else:
            copy(j, 5).wait_recv()

    for tick in range(LAGS[-1] + total):
        for j in range(total):
            if tick - j in LAGS:
                advance(j, LAGS.index(tick - j))
    for j in range(total):
        copy(j, 0).wait_send()
        copy(j, 5).wait_send()

    @pl.when(end)
    def _():
        for j in range(total):
            copy(j, 1).wait_send()

    @pl.when(inner)
    def _():
        for j in range(total):
            for kind in (2, 3, 4):
                copy(j, kind).wait_send()


def token_sums(parts, scale):
    flat = [p.reshape(-1, p.shape[-1]) for p in parts]
    height, width = flat[0].shape
    streams = stream_count(height)
    if lax.axis_size("dp") != 8 or not streams or any(f.shape != flat[0].shape for f in flat):
        return [token_sum(p, scale) for p in parts]
    count, half = len(parts), height // streams // 2
    total = count * streams
    sums = pl.pallas_call(
        functools.partial(sum_streams_body, count, streams, scale),
        out_shape=[jax.ShapeDtypeStruct(f.shape, BF16) for f in flat],
        in_specs=[VM] * count,
        out_specs=[VM] * count,
        scratch_shapes=[
            pltpu.VMEM((total, half, width), F32),
            pltpu.VMEM((total, half, width), BF16),
            pltpu.VMEM((total, half, width), BF16),
            pltpu.VMEM((total, half, width), BF16),
            pltpu.VMEM((total, half // 2, width), BF16),
            pltpu.SemaphoreType.DMA((total, 6)),
            pltpu.SemaphoreType.DMA((total, 6)),
        ],
        compiler_params=pltpu.CompilerParams(
            collective_id=0, has_side_effects=True, vmem_limit_bytes=48 * 2**20
        ),
        cost_estimate=pl.CostEstimate(flops=2**20, bytes_accessed=200 * 2**20, transcendentals=0),
    )(*flat)
    return [s.reshape((1,) + p.shape) for s, p in zip(sums, parts)]


def local(inputs, up_weight, up_pick, down_weight, down_pick, cotangent):
    bit_count = lax.axis_size("mp").bit_length() - 1
    levels = bit_count + 1
    tokens, width = inputs.shape
    in_blocks, slots = down_weight.shape[2:4]
    hid_blocks, size = up_weight.shape[2:4]
    scale = 1.0 / math.sqrt(tokens * lax.axis_size("dp"))
    macs = 2 * levels * hid_blocks * tokens * size * size
    hid = (hid_blocks, tokens, size)
    feat = (in_blocks, tokens, size)

    sources = [inputs] + [swap(inputs, "mp", b) for b in range(bit_count)]
    placed = call(
        functools.partial(back_body, levels),
        [(hid, F32)] + [(hid, BF16)] * bit_count,
        macs, 8 * 2**20, [SM, VM, VM],
        [pltpu.VMEM((levels,) + hid, F32)],
    )(down_pick, cotangent, down_weight)
    grads = [placed[0]] + [swap(placed[b + 1], "mp", b) for b in range(bit_count)]
    hidden, act = call(
        functools.partial(up_body, levels),
        [(hid, F32), (hid, BF16)],
        macs, 8 * 2**20, [SM] + [VM] * (levels + 1),
    )(up_pick, *sources, up_weight)
    acts = [act] + [swap(act, "mp", b) for b in range(bit_count)]
    mid = call(
        functools.partial(mid_body, levels),
        [((levels, hid_blocks, size, size), BF16), (feat, F32)] + [(feat, BF16)] * bit_count,
        2 * macs, 16 * 2**20, [SM] + [VM] * (2 * levels + 2),
        [
            pltpu.VMEM((levels,) + feat, F32),
            pltpu.VMEM((levels, in_blocks, size, tokens), BF16),
        ],
    )(up_pick, *sources, up_weight, hidden, *grads)
    up_part, back = mid[0], mid[1:]
    result, down_part = call(
        functools.partial(down_body, levels),
        [((tokens, width), BF16), ((levels, in_blocks, slots, size, size), BF16)],
        2 * macs, 12 * 2**20, [SM] + [VM] * (levels + 2),
    )(down_pick, *acts, down_weight, cotangent)
    backs = [back[0]] + [swap(back[b + 1], "mp", b) for b in range(bit_count)]
    up_out, down_out = token_sums([up_part, down_part], scale)
    [grad_inputs] = call(
        functools.partial(sum_body, levels),
        [((tokens, width), BF16)], 2**20, 2 * 2**20, [VM] * levels,
    )(*backs)
    return result, grad_inputs, up_out, down_out


def solution(mesh):
    placed = (
        P("dp", "mp"),
        P("mp", None, None, None, None),
        P("mp", None, None),
        P("mp", None, None, None, None, None),
        P("mp", None, None, None),
        P("dp", "mp"),
    )
    return jax.shard_map(
        local,
        mesh=mesh,
        in_specs=placed,
        out_specs=(
            P("dp", "mp"),
            P("dp", "mp"),
            P("mp", None, None, None, None),
            P("mp", None, None, None, None, None),
        ),
        check_vma=False,
    )
```

```python
import functools
import math

import jax
import jax.numpy as jnp
from jax import lax
from jax.experimental import pallas as pl
from jax.experimental.pallas import tpu as pltpu
from jax.sharding import PartitionSpec as P

F32 = jnp.float32
BF16 = jnp.bfloat16
VM = pl.BlockSpec(memory_space=pltpu.VMEM)
SM = pl.BlockSpec(memory_space=pltpu.SMEM)


def dot(a, b, dims):
    return lax.dot_general(a, b, (dims, ((), ())), preferred_element_type=F32)


def call(body, outs, flops, moved, in_specs, scratch=()):
    return pl.pallas_call(
        body,
        out_shape=[jax.ShapeDtypeStruct(s, d) for s, d in outs],
        in_specs=in_specs,
        out_specs=[VM] * len(outs),
        scratch_shapes=list(scratch),
        compiler_params=pltpu.CompilerParams(vmem_limit_bytes=48 * 2**20),
        cost_estimate=pl.CostEstimate(flops=flops, bytes_accessed=moved, transcendentals=0),
    )


def columns(block, size):
    return pl.ds(pl.multiple_of(block * size, size), size)


def back_body(levels, pick, dy, weight, *rest):
    outs, total = rest[:levels], rest[levels]
    _, _, out_blocks, slots, size, _ = weight.shape
    total[...] = jnp.zeros_like(total)

    @pl.loop(0, out_blocks)
    def _(o):
        grad = dy[:, columns(o, size)]
        terms = [
            (l, k, dot(grad, weight[0, l, o, k], ((1,), (1,))))
            for l in range(levels)
            for k in range(slots)
        ]
        for l, k, term in terms:
            spot = pick[0, l, o, k]
            total[l, spot] += term

    for l in range(levels):
        outs[l][...] = total[l].astype(outs[l].dtype)


def gelu_parts(v):
    c = 0.7978845608028654
    t = jnp.tanh(c * (v + 0.044715 * (v * v * v)))
    return t, c


def up_body(levels, pick, *rest):
    sources, weight, hidden, act = rest[:levels], rest[levels], rest[levels + 1], rest[levels + 2]
    hid_blocks, size = weight.shape[2], weight.shape[3]

    def one(o):
        acc = None
        for l in range(levels):
            block = sources[l][:, columns(pick[0, l, o], size)]
            term = dot(block, weight[0, l, o], ((1,), (0,)))
            acc = term if acc is None else acc + term
        t, _ = gelu_parts(acc)
        hidden[o] = acc
        act[o] = (0.5 * acc * (1.0 + t)).astype(BF16)

    @pl.loop(0, hid_blocks // 3)
    def _(step):
        for i in range(3):
            one(step * 3 + i)


def mid_body(levels, pick, *rest):
    sources = rest[:levels]
    weight, hidden = rest[levels], rest[levels + 1]
    grads = rest[levels + 2 : 2 * levels + 2]
    up_part = rest[2 * levels + 2]
    outs = rest[2 * levels + 3 : 3 * levels + 3]
    total, flipped = rest[3 * levels + 3 :]
    hid_blocks, size = weight.shape[2], weight.shape[3]
    in_blocks = sources[0].shape[1] // size
    total[...] = jnp.zeros_like(total)

    @pl.loop(0, in_blocks)
    def _(b):
        for l in range(levels):
            flipped[l, b] = sources[l][:, columns(b, size)].T

    def one(o):
        v = hidden[o]
        grad = grads[0][o]
        for l in range(1, levels):
            grad = grad + grads[l][o].astype(F32)
        t, c = gelu_parts(v)
        slope = 0.5 * (1.0 + t) + 0.5 * v * (1.0 - t * t) * (c * (1.0 + 3 * 0.044715 * (v * v)))
        hg = (grad * slope).astype(BF16)
        terms = []
        for l in range(levels):
            up_part[l, o] = dot(flipped[l, pick[0, l, o]], hg, ((1,), (0,))).astype(BF16)
            terms.append(dot(hg, weight[0, l, o], ((1,), (1,))))
        return terms

    @pl.loop(0, hid_blocks // 2)
    def _(step):
        both = [one(step * 2 + i) for i in range(2)]
        for i in range(2):
            for l in range(levels):
                spot = pick[0, l, step * 2 + i]
                total[l, spot] += both[i][l]

    for l in range(levels):
        outs[l][...] = total[l].astype(outs[l].dtype)


def down_body(levels, pick, *rest):
    acts, weight, dy, result, down_part = rest[:levels], *rest[levels:]
    _, _, out_blocks, slots, size, _ = weight.shape

    @pl.loop(0, out_blocks)
    def _(o):
        grad = dy[:, columns(o, size)]
        acc = None
        for l in range(levels):
            for k in range(slots):
                act = acts[l][pick[0, l, o, k]]
                term = dot(act, weight[0, l, o, k], ((1,), (0,)))
                acc = term if acc is None else acc + term
                down_part[l, o, k] = dot(act, grad, ((0,), (0,))).astype(BF16)
        result[:, columns(o, size)] = acc.astype(BF16)


def sum_body(levels, *rest):
    terms, out = rest[:levels], rest[levels]
    blocks, _, size = terms[0].shape

    for b in range(blocks):
        acc = terms[0][b]
        for l in range(1, levels):
            acc = acc + terms[l][b].astype(F32)
        out[:, b * size : (b + 1) * size] = acc.astype(BF16)


def swap(block, axis, bit):
    count = lax.axis_size(axis)
    return lax.ppermute(block, axis, [(i, i ^ (1 << bit)) for i in range(count)])


def token_sum(part, scale):
    me = lax.axis_index("dp")
    bits = lax.axis_size("dp").bit_length() - 1
    value = part.reshape(-1, part.shape[-1])
    for bit in range(bits):
        mine = (me >> bit) & 1
        rows = value.shape[0] // 2
        sent = lax.dynamic_slice_in_dim(value, (1 - mine) * rows, rows).astype(BF16)
        kept = lax.dynamic_slice_in_dim(value, mine * rows, rows).astype(F32)
        value = kept + swap(sent, "dp", bit).astype(F32)
    value = (value * scale).astype(BF16)
    for bit in reversed(range(bits)):
        mine = (me >> bit) & 1
        other = swap(value, "dp", bit)
        first = jnp.where(mine == 0, value, other)
        last = jnp.where(mine == 0, other, value)
        value = jnp.concatenate([first, last], axis=0)
    return value.reshape((1,) + part.shape)


def stream_count(rows, devices):
    return next((n for n in (6, 4, 3, 2, 1) if rows % (16 * devices * n) == 0), 0)


def sum_streams_body(count, streams, bits, scale, *refs):
    parts, outs = refs[:count], refs[count : 2 * count]
    acc, stage, land, send_sem, recv_sem = refs[2 * count :]
    me = lax.axis_index("dp")
    mine = [lax.rem(lax.div(me, 1 << b), 2) for b in range(bits)]
    peer = [me + (1 - 2 * mine[b]) * (1 << b) for b in range(bits)]
    rows = parts[0].shape[0] // streams
    size = [rows >> (b + 1) for b in range(bits)]
    total = count * streams

    barrier = pltpu.get_barrier_semaphore()
    for b in range(bits):
        pl.semaphore_signal(
            barrier, inc=1, device_id={"dp": peer[b]}, device_id_type=pl.DeviceIdType.MESH
        )
    pl.semaphore_wait(barrier, bits)

    start = [0] * (bits + 1)
    for b in range(bits):
        start[b + 1] = start[b] + mine[b] * size[b]
    place = [0]
    for b in range(bits):
        place.append(place[b] + size[b])

    def span(at, length):
        return pl.ds(pl.multiple_of(at, 16), length)

    def copy(j, step):
        which, base = j // streams, (j % streams) * rows
        if step < bits:
            b = step
            there = start[b] + (1 - mine[b]) * size[b]
            source = (
                parts[which].at[span(base + there, size[0])]
                if b == 0
                else stage.at[j, pl.ds(place[b] - size[0], size[b])]
            )
            target = land.at[j, pl.ds(place[b], size[b])]
        else:
            b = 2 * bits - 1 - step
            source = target = outs[which].at[span(base + start[b + 1], size[b])]
        return pltpu.make_async_remote_copy(
            src_ref=source,
            dst_ref=target,
            send_sem=send_sem.at[j, step],
            recv_sem=recv_sem.at[j, step],
            device_id={"dp": peer[b]},
            device_id_type=pl.DeviceIdType.MESH,
        )

    def advance(j, step):
        which, base = j // streams, (j % streams) * rows
        if step > 0:
            copy(j, step - 1).wait_recv()
        if 0 < step <= bits:
            b = step - 1
            arrived = land[j, pl.ds(place[b], size[b])].astype(jnp.float32)
            if b == 0:
                held = parts[which][span(base + mine[0] * size[0], size[0])].astype(jnp.float32)
            else:
                held = acc[j, span(start[b + 1] - start[1], size[b])]
            value = held + arrived
            if step == bits:
                outs[which][span(base + start[bits], size[b])] = (value * scale).astype(jnp.bfloat16)
            else:
                acc[j, span(start[b + 1] - start[1], size[b])] = value
                away = start[step] - start[1] + (1 - mine[step]) * size[step]
                stage[j, pl.ds(place[step] - size[0], size[step])] = acc[
                    j, span(away, size[step])
                ].astype(jnp.bfloat16)
        if step < 2 * bits:
            copy(j, step).start()

    for tick in range(2 * bits + total):
        for j in range(total):
            if 0 <= tick - j <= 2 * bits:
                advance(j, tick - j)
    for j in range(total):
        for step in range(2 * bits):
            copy(j, step).wait_send()


def token_sums(parts, scale, call_id):
    devices = lax.axis_size("dp")
    bits = devices.bit_length() - 1
    flat = [p.reshape(-1, p.shape[-1]) for p in parts]
    height, width = flat[0].shape
    streams = stream_count(height, devices)
    if not streams or bits < 2 or any(f.shape != flat[0].shape for f in flat):
        return [token_sum(p, scale) for p in parts]
    count, rows = len(parts), height // streams
    total = count * streams
    moved = [rows >> (b + 1) for b in range(bits)]
    sums = pl.pallas_call(
        functools.partial(sum_streams_body, count, streams, bits, scale),
        out_shape=[jax.ShapeDtypeStruct(f.shape, BF16) for f in flat],
        in_specs=[VM] * count,
        out_specs=[VM] * count,
        scratch_shapes=[
            pltpu.VMEM((total, moved[0], width), F32),
            pltpu.VMEM((total, sum(moved[1:]), width), BF16),
            pltpu.VMEM((total, sum(moved), width), BF16),
            pltpu.SemaphoreType.DMA((total, 2 * bits)),
            pltpu.SemaphoreType.DMA((total, 2 * bits)),
        ],
        compiler_params=pltpu.CompilerParams(
            collective_id=call_id, has_side_effects=True, vmem_limit_bytes=48 * 2**20
        ),
        cost_estimate=pl.CostEstimate(flops=2**20, bytes_accessed=200 * 2**20, transcendentals=0),
    )(*flat)
    return [s.reshape((1,) + p.shape) for s, p in zip(sums, parts)]


def local(inputs, up_weight, up_pick, down_weight, down_pick, cotangent):
    bit_count = lax.axis_size("mp").bit_length() - 1
    levels = bit_count + 1
    tokens, width = inputs.shape
    in_blocks, slots = down_weight.shape[2:4]
    hid_blocks, size = up_weight.shape[2:4]
    scale = 1.0 / math.sqrt(tokens * lax.axis_size("dp"))
    macs = 2 * levels * hid_blocks * tokens * size * size
    hid = (hid_blocks, tokens, size)
    feat = (in_blocks, tokens, size)

    sources = [inputs] + [swap(inputs, "mp", b) for b in range(bit_count)]
    placed = call(
        functools.partial(back_body, levels),
        [(hid, F32)] + [(hid, BF16)] * bit_count,
        macs, 8 * 2**20, [SM, VM, VM],
        [pltpu.VMEM((levels,) + hid, F32)],
    )(down_pick, cotangent, down_weight)
    grads = [placed[0]] + [swap(placed[b + 1], "mp", b) for b in range(bit_count)]
    hidden, act = call(
        functools.partial(up_body, levels),
        [(hid, F32), (hid, BF16)],
        macs, 8 * 2**20, [SM] + [VM] * (levels + 1),
    )(up_pick, *sources, up_weight)
    acts = [act] + [swap(act, "mp", b) for b in range(bit_count)]
    mid = call(
        functools.partial(mid_body, levels),
        [((levels, hid_blocks, size, size), BF16), (feat, F32)] + [(feat, BF16)] * bit_count,
        2 * macs, 16 * 2**20, [SM] + [VM] * (2 * levels + 2),
        [
            pltpu.VMEM((levels,) + feat, F32),
            pltpu.VMEM((levels, in_blocks, size, tokens), BF16),
        ],
    )(up_pick, *sources, up_weight, hidden, *grads)
    up_part, back = mid[0], mid[1:]
    backs = [back[0]] + [swap(back[b + 1], "mp", b) for b in range(bit_count)]
    [up_out] = token_sums([up_part], scale, 0)
    up_out, down_pick = lax.optimization_barrier((up_out, down_pick))
    result, down_part = call(
        functools.partial(down_body, levels),
        [((tokens, width), BF16), ((levels, in_blocks, slots, size, size), BF16)],
        2 * macs, 12 * 2**20, [SM] + [VM] * (levels + 2),
    )(down_pick, *acts, down_weight, cotangent)
    [down_out] = token_sums([down_part], scale, 1)
    [grad_inputs] = call(
        functools.partial(sum_body, levels),
        [((tokens, width), BF16)], 2**20, 2 * 2**20, [VM] * levels,
    )(*backs)
    return result, grad_inputs, up_out, down_out


def solution(mesh):
    placed = (
        P("dp", "mp"),
        P("mp", None, None, None, None),
        P("mp", None, None),
        P("mp", None, None, None, None, None),
        P("mp", None, None, None),
        P("dp", "mp"),
    )
    return jax.shard_map(
        local,
        mesh=mesh,
        in_specs=placed,
        out_specs=(
            P("dp", "mp"),
            P("dp", "mp"),
            P("mp", None, None, None, None),
            P("mp", None, None, None, None, None),
        ),
        check_vma=False,
    )
```

```python
import functools
import math

import jax
import jax.numpy as jnp
from jax import lax
from jax.experimental import pallas as pl
from jax.experimental.pallas import tpu as pltpu
from jax.sharding import PartitionSpec as P

F32 = jnp.float32
BF16 = jnp.bfloat16
VM = pl.BlockSpec(memory_space=pltpu.VMEM)
SM = pl.BlockSpec(memory_space=pltpu.SMEM)


def dot(a, b, dims):
    return lax.dot_general(a, b, (dims, ((), ())), preferred_element_type=F32)


def call(body, outs, flops, moved, in_specs, scratch=()):
    return pl.pallas_call(
        body,
        out_shape=[jax.ShapeDtypeStruct(s, d) for s, d in outs],
        in_specs=in_specs,
        out_specs=[VM] * len(outs),
        scratch_shapes=list(scratch),
        compiler_params=pltpu.CompilerParams(vmem_limit_bytes=48 * 2**20),
        cost_estimate=pl.CostEstimate(flops=flops, bytes_accessed=moved, transcendentals=0),
    )


def columns(block, size):
    return pl.ds(pl.multiple_of(block * size, size), size)


def back_body(levels, pick, dy, weight, *rest):
    outs, total = rest[:levels], rest[levels]
    _, _, out_blocks, slots, size, _ = weight.shape
    total[...] = jnp.zeros_like(total)

    @pl.loop(0, out_blocks)
    def _(o):
        grad = dy[:, columns(o, size)]
        terms = [
            (l, k, dot(grad, weight[0, l, o, k], ((1,), (1,))))
            for l in range(levels)
            for k in range(slots)
        ]
        for l, k, term in terms:
            spot = pick[0, l, o, k]
            total[l, spot] += term

    for l in range(levels):
        outs[l][...] = total[l].astype(outs[l].dtype)


def gelu_parts(v):
    c = 0.7978845608028654
    t = jnp.tanh(c * (v + 0.044715 * (v * v * v)))
    return t, c


def up_body(levels, pick, *rest):
    sources, weight, hidden, act = rest[:levels], rest[levels], rest[levels + 1], rest[levels + 2]
    hid_blocks, size = weight.shape[2], weight.shape[3]

    def one(o):
        acc = None
        for l in range(levels):
            block = sources[l][:, columns(pick[0, l, o], size)]
            term = dot(block, weight[0, l, o], ((1,), (0,)))
            acc = term if acc is None else acc + term
        t, _ = gelu_parts(acc)
        hidden[o] = acc
        act[o] = (0.5 * acc * (1.0 + t)).astype(BF16)

    @pl.loop(0, hid_blocks // 3)
    def _(step):
        for i in range(3):
            one(step * 3 + i)


def mid_body(levels, pick, *rest):
    sources = rest[:levels]
    weight, hidden = rest[levels], rest[levels + 1]
    grads = rest[levels + 2 : 2 * levels + 2]
    up_part = rest[2 * levels + 2]
    outs = rest[2 * levels + 3 : 3 * levels + 3]
    total, flipped = rest[3 * levels + 3 :]
    hid_blocks, size = weight.shape[2], weight.shape[3]
    in_blocks = sources[0].shape[1] // size
    total[...] = jnp.zeros_like(total)

    @pl.loop(0, in_blocks)
    def _(b):
        for l in range(levels):
            flipped[l, b] = sources[l][:, columns(b, size)].T

    def one(o):
        v = hidden[o]
        grad = grads[0][o]
        for l in range(1, levels):
            grad = grad + grads[l][o].astype(F32)
        t, c = gelu_parts(v)
        slope = 0.5 * (1.0 + t) + 0.5 * v * (1.0 - t * t) * (c * (1.0 + 3 * 0.044715 * (v * v)))
        hg = (grad * slope).astype(BF16)
        terms = []
        for l in range(levels):
            up_part[l, o] = dot(flipped[l, pick[0, l, o]], hg, ((1,), (0,))).astype(BF16)
            terms.append(dot(hg, weight[0, l, o], ((1,), (1,))))
        return terms

    @pl.loop(0, hid_blocks // 2)
    def _(step):
        both = [one(step * 2 + i) for i in range(2)]
        for i in range(2):
            for l in range(levels):
                spot = pick[0, l, step * 2 + i]
                total[l, spot] += both[i][l]

    for l in range(levels):
        outs[l][...] = total[l].astype(outs[l].dtype)


def down_body(levels, pick, *rest):
    acts, weight, dy, result, down_part = rest[:levels], *rest[levels:]
    _, _, out_blocks, slots, size, _ = weight.shape

    @pl.loop(0, out_blocks)
    def _(o):
        grad = dy[:, columns(o, size)]
        acc = None
        for l in range(levels):
            for k in range(slots):
                act = acts[l][pick[0, l, o, k]]
                term = dot(act, weight[0, l, o, k], ((1,), (0,)))
                acc = term if acc is None else acc + term
                down_part[l, o, k] = dot(act, grad, ((0,), (0,))).astype(BF16)
        result[:, columns(o, size)] = acc.astype(BF16)


def sum_body(levels, *rest):
    terms, out = rest[:levels], rest[levels]
    blocks, _, size = terms[0].shape

    for b in range(blocks):
        acc = terms[0][b]
        for l in range(1, levels):
            acc = acc + terms[l][b].astype(F32)
        out[:, b * size : (b + 1) * size] = acc.astype(BF16)


def swap(block, axis, bit):
    count = lax.axis_size(axis)
    return lax.ppermute(block, axis, [(i, i ^ (1 << bit)) for i in range(count)])


def token_sum(part, scale):
    me = lax.axis_index("dp")
    bits = lax.axis_size("dp").bit_length() - 1
    value = part.reshape(-1, part.shape[-1])
    for bit in range(bits):
        mine = (me >> bit) & 1
        rows = value.shape[0] // 2
        sent = lax.dynamic_slice_in_dim(value, (1 - mine) * rows, rows).astype(BF16)
        kept = lax.dynamic_slice_in_dim(value, mine * rows, rows).astype(F32)
        value = kept + swap(sent, "dp", bit).astype(F32)
    value = (value * scale).astype(BF16)
    for bit in reversed(range(bits)):
        mine = (me >> bit) & 1
        other = swap(value, "dp", bit)
        first = jnp.where(mine == 0, value, other)
        last = jnp.where(mine == 0, other, value)
        value = jnp.concatenate([first, last], axis=0)
    return value.reshape((1,) + part.shape)


def stream_count(rows, devices):
    return next((n for n in (6, 4, 3, 2, 1) if rows % (16 * devices * n) == 0), 0)


def sum_streams_body(count, streams, bits, scale, *refs):
    parts, outs = refs[:count], refs[count : 2 * count]
    acc, stage, land, send_sem, recv_sem = refs[2 * count :]
    me = lax.axis_index("dp")
    mine = [lax.rem(lax.div(me, 1 << b), 2) for b in range(bits)]
    peer = [me + (1 - 2 * mine[b]) * (1 << b) for b in range(bits)]
    rows = parts[0].shape[0] // streams
    size = [rows >> (b + 1) for b in range(bits)]
    total = count * streams

    barrier = pltpu.get_barrier_semaphore()
    for b in range(bits):
        pl.semaphore_signal(
            barrier, inc=1, device_id={"dp": peer[b]}, device_id_type=pl.DeviceIdType.MESH
        )
    pl.semaphore_wait(barrier, bits)

    start = [0] * (bits + 1)
    for b in range(bits):
        start[b + 1] = start[b] + mine[b] * size[b]
    place = [0]
    for b in range(bits):
        place.append(place[b] + size[b])

    def span(at, length):
        return pl.ds(pl.multiple_of(at, 16), length)

    def copy(j, step):
        which, base = j // streams, (j % streams) * rows
        if step < bits:
            b = step
            there = start[b] + (1 - mine[b]) * size[b]
            source = (
                parts[which].at[span(base + there, size[0])]
                if b == 0
                else stage.at[j, pl.ds(place[b] - size[0], size[b])]
            )
            target = land.at[j, pl.ds(place[b], size[b])]
        else:
            b = 2 * bits - 1 - step
            source = target = outs[which].at[span(base + start[b + 1], size[b])]
        return pltpu.make_async_remote_copy(
            src_ref=source,
            dst_ref=target,
            send_sem=send_sem.at[j, step],
            recv_sem=recv_sem.at[j, step],
            device_id={"dp": peer[b]},
            device_id_type=pl.DeviceIdType.MESH,
        )

    def advance(j, step):
        which, base = j // streams, (j % streams) * rows
        if step > 0:
            copy(j, step - 1).wait_recv()
        if 0 < step <= bits:
            b = step - 1
            arrived = land[j, pl.ds(place[b], size[b])].astype(jnp.float32)
            if b == 0:
                held = parts[which][span(base + mine[0] * size[0], size[0])].astype(jnp.float32)
            else:
                held = acc[j, span(start[b + 1] - start[1], size[b])]
            value = held + arrived
            if step == bits:
                outs[which][span(base + start[bits], size[b])] = (value * scale).astype(jnp.bfloat16)
            else:
                acc[j, span(start[b + 1] - start[1], size[b])] = value
                away = start[step] - start[1] + (1 - mine[step]) * size[step]
                stage[j, pl.ds(place[step] - size[0], size[step])] = acc[
                    j, span(away, size[step])
                ].astype(jnp.bfloat16)
        if step < 2 * bits:
            copy(j, step).start()

    for tick in range(4 * bits + total):
        for j in range(total):
            if 0 <= tick - j <= 4 * bits and (tick - j) % 2 == 0:
                advance(j, (tick - j) // 2)
    for j in range(total):
        for step in range(2 * bits):
            copy(j, step).wait_send()


def token_sums(parts, scale):
    devices = lax.axis_size("dp")
    bits = devices.bit_length() - 1
    flat = [p.reshape(-1, p.shape[-1]) for p in parts]
    height, width = flat[0].shape
    streams = stream_count(height, devices)
    if not streams or bits < 2 or any(f.shape != flat[0].shape for f in flat):
        return [token_sum(p, scale) for p in parts]
    count, rows = len(parts), height // streams
    total = count * streams
    moved = [rows >> (b + 1) for b in range(bits)]
    sums = pl.pallas_call(
        functools.partial(sum_streams_body, count, streams, bits, scale),
        out_shape=[jax.ShapeDtypeStruct(f.shape, BF16) for f in flat],
        in_specs=[VM] * count,
        out_specs=[VM] * count,
        scratch_shapes=[
            pltpu.VMEM((total, moved[0], width), F32),
            pltpu.VMEM((total, sum(moved[1:]), width), BF16),
            pltpu.VMEM((total, sum(moved), width), BF16),
            pltpu.SemaphoreType.DMA((total, 2 * bits)),
            pltpu.SemaphoreType.DMA((total, 2 * bits)),
        ],
        compiler_params=pltpu.CompilerParams(
            collective_id=0, has_side_effects=True, vmem_limit_bytes=48 * 2**20
        ),
        cost_estimate=pl.CostEstimate(flops=2**20, bytes_accessed=200 * 2**20, transcendentals=0),
    )(*flat)
    return [s.reshape((1,) + p.shape) for s, p in zip(sums, parts)]


def local(inputs, up_weight, up_pick, down_weight, down_pick, cotangent):
    bit_count = lax.axis_size("mp").bit_length() - 1
    levels = bit_count + 1
    tokens, width = inputs.shape
    in_blocks, slots = down_weight.shape[2:4]
    hid_blocks, size = up_weight.shape[2:4]
    scale = 1.0 / math.sqrt(tokens * lax.axis_size("dp"))
    macs = 2 * levels * hid_blocks * tokens * size * size
    hid = (hid_blocks, tokens, size)
    feat = (in_blocks, tokens, size)

    sources = [inputs] + [swap(inputs, "mp", b) for b in range(bit_count)]
    placed = call(
        functools.partial(back_body, levels),
        [(hid, F32)] + [(hid, BF16)] * bit_count,
        macs, 8 * 2**20, [SM, VM, VM],
        [pltpu.VMEM((levels,) + hid, F32)],
    )(down_pick, cotangent, down_weight)
    grads = [placed[0]] + [swap(placed[b + 1], "mp", b) for b in range(bit_count)]
    hidden, act = call(
        functools.partial(up_body, levels),
        [(hid, F32), (hid, BF16)],
        macs, 8 * 2**20, [SM] + [VM] * (levels + 1),
    )(up_pick, *sources, up_weight)
    acts = [act] + [swap(act, "mp", b) for b in range(bit_count)]
    mid = call(
        functools.partial(mid_body, levels),
        [((levels, hid_blocks, size, size), BF16), (feat, F32)] + [(feat, BF16)] * bit_count,
        2 * macs, 16 * 2**20, [SM] + [VM] * (2 * levels + 2),
        [
            pltpu.VMEM((levels,) + feat, F32),
            pltpu.VMEM((levels, in_blocks, size, tokens), BF16),
        ],
    )(up_pick, *sources, up_weight, hidden, *grads)
    up_part, back = mid[0], mid[1:]
    result, down_part = call(
        functools.partial(down_body, levels),
        [((tokens, width), BF16), ((levels, in_blocks, slots, size, size), BF16)],
        2 * macs, 12 * 2**20, [SM] + [VM] * (levels + 2),
    )(down_pick, *acts, down_weight, cotangent)
    backs = [back[0]] + [swap(back[b + 1], "mp", b) for b in range(bit_count)]
    up_out, down_out = token_sums([up_part, down_part], scale)
    [grad_inputs] = call(
        functools.partial(sum_body, levels),
        [((tokens, width), BF16)], 2**20, 2 * 2**20, [VM] * levels,
    )(*backs)
    return result, grad_inputs, up_out, down_out


def solution(mesh):
    placed = (
        P("dp", "mp"),
        P("mp", None, None, None, None),
        P("mp", None, None),
        P("mp", None, None, None, None, None),
        P("mp", None, None, None),
        P("dp", "mp"),
    )
    return jax.shard_map(
        local,
        mesh=mesh,
        in_specs=placed,
        out_specs=(
            P("dp", "mp"),
            P("dp", "mp"),
            P("mp", None, None, None, None),
            P("mp", None, None, None, None, None),
        ),
        check_vma=False,
    )
```

```python
import functools
import math

import jax
import jax.numpy as jnp
from jax import lax
from jax.experimental import pallas as pl
from jax.experimental.pallas import tpu as pltpu
from jax.sharding import PartitionSpec as P

F32 = jnp.float32
BF16 = jnp.bfloat16
VM = pl.BlockSpec(memory_space=pltpu.VMEM)
SM = pl.BlockSpec(memory_space=pltpu.SMEM)


def dot(a, b, dims):
    return lax.dot_general(a, b, (dims, ((), ())), preferred_element_type=F32)


def call(body, outs, flops, moved, in_specs, scratch=()):
    return pl.pallas_call(
        body,
        out_shape=[jax.ShapeDtypeStruct(s, d) for s, d in outs],
        in_specs=in_specs,
        out_specs=[VM] * len(outs),
        scratch_shapes=list(scratch),
        compiler_params=pltpu.CompilerParams(vmem_limit_bytes=48 * 2**20),
        cost_estimate=pl.CostEstimate(flops=flops, bytes_accessed=moved, transcendentals=0),
    )


def columns(block, size):
    return pl.ds(pl.multiple_of(block * size, size), size)


def back_body(levels, pick, dy, weight, *rest):
    outs, total = rest[:levels], rest[levels]
    _, _, out_blocks, slots, size, _ = weight.shape
    total[...] = jnp.zeros_like(total)

    @pl.loop(0, out_blocks)
    def _(o):
        grad = dy[:, columns(o, size)]
        terms = [
            (l, k, dot(grad, weight[0, l, o, k], ((1,), (1,))))
            for l in range(levels)
            for k in range(slots)
        ]
        for l, k, term in terms:
            spot = pick[0, l, o, k]
            total[l, spot] += term

    for l in range(levels):
        outs[l][...] = total[l].astype(outs[l].dtype)


def gelu_parts(v):
    c = 0.7978845608028654
    t = jnp.tanh(c * (v + 0.044715 * (v * v * v)))
    return t, c


def up_body(levels, pick, *rest):
    sources, weight, hidden, act = rest[:levels], rest[levels], rest[levels + 1], rest[levels + 2]
    hid_blocks, size = weight.shape[2], weight.shape[3]

    def one(o):
        acc = None
        for l in range(levels):
            block = sources[l][:, columns(pick[0, l, o], size)]
            term = dot(block, weight[0, l, o], ((1,), (0,)))
            acc = term if acc is None else acc + term
        t, _ = gelu_parts(acc)
        hidden[o] = acc
        act[o] = (0.5 * acc * (1.0 + t)).astype(BF16)

    @pl.loop(0, hid_blocks // 3)
    def _(step):
        for i in range(3):
            one(step * 3 + i)


def mid_body(levels, pick, *rest):
    sources = rest[:levels]
    weight, hidden = rest[levels], rest[levels + 1]
    grads = rest[levels + 2 : 2 * levels + 2]
    up_part = rest[2 * levels + 2]
    outs = rest[2 * levels + 3 : 3 * levels + 3]
    total, flipped = rest[3 * levels + 3 :]
    hid_blocks, size = weight.shape[2], weight.shape[3]
    in_blocks = sources[0].shape[1] // size
    total[...] = jnp.zeros_like(total)

    @pl.loop(0, in_blocks)
    def _(b):
        for l in range(levels):
            flipped[l, b] = sources[l][:, columns(b, size)].T

    def one(o):
        v = hidden[o]
        grad = grads[0][o]
        for l in range(1, levels):
            grad = grad + grads[l][o].astype(F32)
        t, c = gelu_parts(v)
        slope = 0.5 * (1.0 + t) + 0.5 * v * (1.0 - t * t) * (c * (1.0 + 3 * 0.044715 * (v * v)))
        hg = (grad * slope).astype(BF16)
        terms = []
        for l in range(levels):
            up_part[l, o] = dot(flipped[l, pick[0, l, o]], hg, ((1,), (0,))).astype(BF16)
            terms.append(dot(hg, weight[0, l, o], ((1,), (1,))))
        return terms

    @pl.loop(0, hid_blocks // 2)
    def _(step):
        both = [one(step * 2 + i) for i in range(2)]
        for i in range(2):
            for l in range(levels):
                spot = pick[0, l, step * 2 + i]
                total[l, spot] += both[i][l]

    for l in range(levels):
        outs[l][...] = total[l].astype(outs[l].dtype)


def down_body(levels, pick, *rest):
    acts, weight, dy, result, down_part = rest[:levels], *rest[levels:]
    _, _, out_blocks, slots, size, _ = weight.shape

    @pl.loop(0, out_blocks)
    def _(o):
        grad = dy[:, columns(o, size)]
        acc = None
        for l in range(levels):
            for k in range(slots):
                act = acts[l][pick[0, l, o, k]]
                term = dot(act, weight[0, l, o, k], ((1,), (0,)))
                acc = term if acc is None else acc + term
                down_part[l, o, k] = dot(act, grad, ((0,), (0,))).astype(BF16)
        result[:, columns(o, size)] = acc.astype(BF16)


def sum_body(levels, *rest):
    terms, out = rest[:levels], rest[levels]
    blocks, _, size = terms[0].shape

    for b in range(blocks):
        acc = terms[0][b]
        for l in range(1, levels):
            acc = acc + terms[l][b].astype(F32)
        out[:, b * size : (b + 1) * size] = acc.astype(BF16)


def swap(block, axis, bit):
    count = lax.axis_size(axis)
    return lax.ppermute(block, axis, [(i, i ^ (1 << bit)) for i in range(count)])


def token_sum(part, scale):
    me = lax.axis_index("dp")
    bits = lax.axis_size("dp").bit_length() - 1
    value = part.reshape(-1, part.shape[-1])
    for bit in range(bits):
        mine = (me >> bit) & 1
        rows = value.shape[0] // 2
        sent = lax.dynamic_slice_in_dim(value, (1 - mine) * rows, rows).astype(BF16)
        kept = lax.dynamic_slice_in_dim(value, mine * rows, rows).astype(F32)
        value = kept + swap(sent, "dp", bit).astype(F32)
    value = (value * scale).astype(BF16)
    for bit in reversed(range(bits)):
        mine = (me >> bit) & 1
        other = swap(value, "dp", bit)
        first = jnp.where(mine == 0, value, other)
        last = jnp.where(mine == 0, other, value)
        value = jnp.concatenate([first, last], axis=0)
    return value.reshape((1,) + part.shape)


def stream_count(rows, devices):
    return next((n for n in (8, 6, 4, 3, 2, 1) if rows % (16 * devices * n) == 0), 0)


def sum_streams_body(count, streams, bits, scale, *refs):
    parts, outs = refs[:count], refs[count : 2 * count]
    acc, stage, land, send_sem, recv_sem = refs[2 * count :]
    me = lax.axis_index("dp")
    mine = [lax.rem(lax.div(me, 1 << b), 2) for b in range(bits)]
    peer = [me + (1 - 2 * mine[b]) * (1 << b) for b in range(bits)]
    rows = parts[0].shape[0] // streams
    size = [rows >> (b + 1) for b in range(bits)]
    total = count * streams

    barrier = pltpu.get_barrier_semaphore()
    for b in range(bits):
        pl.semaphore_signal(
            barrier, inc=1, device_id={"dp": peer[b]}, device_id_type=pl.DeviceIdType.MESH
        )
    pl.semaphore_wait(barrier, bits)

    start = [0] * (bits + 1)
    for b in range(bits):
        start[b + 1] = start[b] + mine[b] * size[b]
    place = [0]
    for b in range(bits):
        place.append(place[b] + size[b])

    def span(at, length):
        return pl.ds(pl.multiple_of(at, 16), length)

    def copy(j, step):
        which, base = j // streams, (j % streams) * rows
        if step < bits:
            b = step
            there = start[b] + (1 - mine[b]) * size[b]
            source = (
                parts[which].at[span(base + there, size[0])]
                if b == 0
                else stage.at[j, pl.ds(place[b] - size[0], size[b])]
            )
            target = land.at[j, pl.ds(place[b], size[b])]
        else:
            b = 2 * bits - 1 - step
            source = target = outs[which].at[span(base + start[b + 1], size[b])]
        return pltpu.make_async_remote_copy(
            src_ref=source,
            dst_ref=target,
            send_sem=send_sem.at[j, step],
            recv_sem=recv_sem.at[j, step],
            device_id={"dp": peer[b]},
            device_id_type=pl.DeviceIdType.MESH,
        )

    def advance(j, step):
        which, base = j // streams, (j % streams) * rows
        if step > 0:
            copy(j, step - 1).wait_recv()
        if 0 < step <= bits:
            b = step - 1
            arrived = land[j, pl.ds(place[b], size[b])].astype(jnp.float32)
            if b == 0:
                held = parts[which][span(base + mine[0] * size[0], size[0])].astype(jnp.float32)
            else:
                held = acc[j, span(start[b + 1] - start[1], size[b])]
            value = held + arrived
            if step == bits:
                outs[which][span(base + start[bits], size[b])] = (value * scale).astype(jnp.bfloat16)
            else:
                acc[j, span(start[b + 1] - start[1], size[b])] = value
                away = start[step] - start[1] + (1 - mine[step]) * size[step]
                stage[j, pl.ds(place[step] - size[0], size[step])] = acc[
                    j, span(away, size[step])
                ].astype(jnp.bfloat16)
        if step < 2 * bits:
            copy(j, step).start()

    for tick in range(4 * bits + total):
        for j in range(total):
            if 0 <= tick - j <= 4 * bits and (tick - j) % 2 == 0:
                advance(j, (tick - j) // 2)
    for j in range(total):
        for step in range(2 * bits):
            copy(j, step).wait_send()


def token_sums(parts, scale):
    devices = lax.axis_size("dp")
    bits = devices.bit_length() - 1
    flat = [p.reshape(-1, p.shape[-1]) for p in parts]
    height, width = flat[0].shape
    streams = stream_count(height, devices)
    if not streams or bits < 2 or any(f.shape != flat[0].shape for f in flat):
        return [token_sum(p, scale) for p in parts]
    count, rows = len(parts), height // streams
    total = count * streams
    moved = [rows >> (b + 1) for b in range(bits)]
    sums = pl.pallas_call(
        functools.partial(sum_streams_body, count, streams, bits, scale),
        out_shape=[jax.ShapeDtypeStruct(f.shape, BF16) for f in flat],
        in_specs=[VM] * count,
        out_specs=[VM] * count,
        scratch_shapes=[
            pltpu.VMEM((total, moved[0], width), F32),
            pltpu.VMEM((total, sum(moved[1:]), width), BF16),
            pltpu.VMEM((total, sum(moved), width), BF16),
            pltpu.SemaphoreType.DMA((total, 2 * bits)),
            pltpu.SemaphoreType.DMA((total, 2 * bits)),
        ],
        compiler_params=pltpu.CompilerParams(
            collective_id=0, has_side_effects=True, vmem_limit_bytes=48 * 2**20
        ),
        cost_estimate=pl.CostEstimate(flops=2**20, bytes_accessed=200 * 2**20, transcendentals=0),
    )(*flat)
    return [s.reshape((1,) + p.shape) for s, p in zip(sums, parts)]


def local(inputs, up_weight, up_pick, down_weight, down_pick, cotangent):
    bit_count = lax.axis_size("mp").bit_length() - 1
    levels = bit_count + 1
    tokens, width = inputs.shape
    in_blocks, slots = down_weight.shape[2:4]
    hid_blocks, size = up_weight.shape[2:4]
    scale = 1.0 / math.sqrt(tokens * lax.axis_size("dp"))
    macs = 2 * levels * hid_blocks * tokens * size * size
    hid = (hid_blocks, tokens, size)
    feat = (in_blocks, tokens, size)

    sources = [inputs] + [swap(inputs, "mp", b) for b in range(bit_count)]
    placed = call(
        functools.partial(back_body, levels),
        [(hid, F32)] + [(hid, BF16)] * bit_count,
        macs, 8 * 2**20, [SM, VM, VM],
        [pltpu.VMEM((levels,) + hid, F32)],
    )(down_pick, cotangent, down_weight)
    grads = [placed[0]] + [swap(placed[b + 1], "mp", b) for b in range(bit_count)]
    hidden, act = call(
        functools.partial(up_body, levels),
        [(hid, F32), (hid, BF16)],
        macs, 8 * 2**20, [SM] + [VM] * (levels + 1),
    )(up_pick, *sources, up_weight)
    acts = [act] + [swap(act, "mp", b) for b in range(bit_count)]
    mid = call(
        functools.partial(mid_body, levels),
        [((levels, hid_blocks, size, size), BF16), (feat, F32)] + [(feat, BF16)] * bit_count,
        2 * macs, 16 * 2**20, [SM] + [VM] * (2 * levels + 2),
        [
            pltpu.VMEM((levels,) + feat, F32),
            pltpu.VMEM((levels, in_blocks, size, tokens), BF16),
        ],
    )(up_pick, *sources, up_weight, hidden, *grads)
    up_part, back = mid[0], mid[1:]
    result, down_part = call(
        functools.partial(down_body, levels),
        [((tokens, width), BF16), ((levels, in_blocks, slots, size, size), BF16)],
        2 * macs, 12 * 2**20, [SM] + [VM] * (levels + 2),
    )(down_pick, *acts, down_weight, cotangent)
    backs = [back[0]] + [swap(back[b + 1], "mp", b) for b in range(bit_count)]
    up_out, down_out = token_sums([up_part, down_part], scale)
    [grad_inputs] = call(
        functools.partial(sum_body, levels),
        [((tokens, width), BF16)], 2**20, 2 * 2**20, [VM] * levels,
    )(*backs)
    return result, grad_inputs, up_out, down_out


def solution(mesh):
    placed = (
        P("dp", "mp"),
        P("mp", None, None, None, None),
        P("mp", None, None),
        P("mp", None, None, None, None, None),
        P("mp", None, None, None),
        P("dp", "mp"),
    )
    return jax.shard_map(
        local,
        mesh=mesh,
        in_specs=placed,
        out_specs=(
            P("dp", "mp"),
            P("dp", "mp"),
            P("mp", None, None, None, None),
            P("mp", None, None, None, None, None),
        ),
        check_vma=False,
    )
```
